32 devices in a mesh: groups: 2 (over x), chan: 16 (over z, y, core).
Axes of the slice: x: 2, y: 2, z: 4, core: 2. Of those that a mesh axis runs over, the one named last changes fastest.
Arguments:
- spectra: bfloat16 [32, 2, 2, 64, 4096], P(('groups', 'chan')), parts along dimension 0, may hold values from -6 to 6
- pair_valid: int32 [32, 8], P(('groups', 'chan')), parts along dimension 0, may hold values from 0 to 1, as said below
Outputs:
- correlations: float32 [32, 8, 64, 512], P(('groups', 'chan')), parts along dimension 0
The draws below stay inside these ranges and needn't reach their ends.
There are 2 independent parts, one for each index of `groups`. The reference program is written for one: setup_inputs(seed, part) draws one part's arguments, and reference() takes and returns one part's arrays. A program takes and returns all parts, laid end to end along the dimension named above; each array names one. Nothing has to cross between parts.
Inputs may be any that keep to these rules, and one draw needn't show every extreme that they name: pair_valid[b,0] is 1 for every block.
All inputs are finite; a program needn't handle non-finite values.
Results may differ from the reference program's by a relative error of at most 0.0034.
Values may be sent and summed in bfloat16 or wider, within the bound.
No kernel may reach another device: no remote copies, remote signals or barrier semaphores. Data moves between devices by JAX's collectives and lax.ppermute only.
A program may use at most 128 MiB of HBM per device.

```python
import math
import jax
import jax.numpy as jnp
from jax import lax

F = 4096
CB = 64
SEG = 2
LAGS = 8
STEPS = 8
NB = 16
STRIDE = 1


def draw_pair_valid(key, part):
    key = jax.random.fold_in(key, 11)
    key_level, key_roll = jax.random.split(key)
    levels = jax.random.randint(key_level, (NB, 1), 5, 96)
    rolls = jax.random.randint(key_roll, (NB, STEPS), 0, 100)
    flags = (rolls < levels).astype(jnp.int32)
    return flags.at[:, 0].set(1)


def steps_of(stream_key, extent, cuts, low, largest):
    factor_of = 1.0
    for axis_at, shards_of in cuts:
        heights = jax.random.uniform(jax.random.fold_in(jax.random.fold_in(stream_key, 6), axis_at), (shards_of,), jnp.float32, low / len(cuts), largest / len(cuts))
        factor_of = factor_of * jnp.repeat(jnp.exp(heights), extent[axis_at] // shards_of).reshape((-1,) + (1,) * (len(extent) - 1 - axis_at))
    return factor_of


def gaussian(key, shape, deviation, reach, cuts=(), kind=jnp.bfloat16):
    array = deviation * jax.random.normal(key, shape, jnp.float32)
    if cuts:
        array = array * steps_of(key, shape, cuts, -0.22, 0.18)
    return jnp.clip(array, -reach, reach).astype(kind)


def setup_inputs(seed: int = 0, part: int = 0) -> dict:
    key_list = jax.random.split(jax.random.key(seed), 3)
    part_splits = jax.random.split(jax.random.fold_in(key_list[2], part), 3)
    spectra = gaussian(part_splits[0], (NB, SEG, 2, CB, F), 1.0, 6.0, ((0, 16),))
    pair_valid = draw_pair_valid(jax.random.fold_in(jax.random.fold_in(key_list[2], part), 71), part)
    return dict(spectra=spectra, pair_valid=pair_valid)


def lag_table(bins, lags):
    freq = jnp.arange(bins, dtype=jnp.int32)[:, None]
    shift = jnp.arange(lags, dtype=jnp.int32)[None, :] - lags // 2
    phase = jnp.mod(freq * shift, 2 * bins)
    angle = phase.astype(jnp.float32) * (math.pi / bins)
    return jnp.concatenate([jnp.cos(angle), -jnp.sin(angle)], 0).astype(jnp.bfloat16)

def modulate(own, table, bins):
    cosine = table[:bins].astype(jnp.float32).T
    sine = table[bins:].astype(jnp.float32).T
    real_part = own[:, 0].astype(jnp.float32)[:, :, None, :]
    imag_part = own[:, 1].astype(jnp.float32)[:, :, None, :]
    first = real_part * cosine[None, None] + imag_part * sine[None, None]
    second = imag_part * cosine[None, None] - real_part * sine[None, None]
    stacked = jnp.stack([first, second], 1)
    return jnp.transpose(stacked, (2, 3, 0, 1, 4)).astype(jnp.bfloat16)

def reference(spectra, pair_valid):
    table = lag_table(F, LAGS)
    norm = 1.0 / math.sqrt(2.0 * SEG * F)

    def one_block(block):
        own = spectra[block]
        modulated = modulate(own, table, F).astype(jnp.float32)
        sources = jnp.mod(block - STRIDE * jnp.arange(STEPS, dtype=jnp.int32), NB).astype(jnp.int32)

        def one_pair(source):
            other = spectra[source].astype(jnp.float32)
            return jnp.einsum('itscf,scjf->itj', modulated, other).reshape(CB, LAGS * CB)
        result = lax.map(one_pair, sources)
        weight = pair_valid[block].astype(jnp.float32) * norm
        return result * weight[:, None, None]
    return lax.map(one_block, jnp.arange(NB, dtype=jnp.int32))
```

```python
import functools
import math

import jax
import jax.numpy as jnp
import ml_dtypes
import numpy as np
from jax import lax
from jax.experimental import pallas as pl
from jax.experimental.pallas import tpu as pltpu
from jax.sharding import PartitionSpec as P

PLANE = 4


def lag_rows(bins, lags):
    rows = np.arange(8)[:, None]
    phase = np.mod(np.arange(bins)[None, :] * rows, 2 * bins)
    angle = phase.astype(np.float64) * (math.pi / bins)
    def rounded(x):
        return x.astype(np.float32).astype(ml_dtypes.bfloat16).astype(np.float32)
    return rounded(np.cos(angle)), rounded(np.sin(angle))


def pair_kernel(lags, steps, first, count, cols_ref, half_ref, *refs):
    own = refs[:PLANE]
    other = refs[PLANE:PLANE + count]
    cos_ref, sin_ref = refs[PLANE + count:PLANE + count + 2]
    outs = refs[PLANE + count + 2:2 * PLANE + count + 2]
    rhs, mod, acc = refs[2 * PLANE + count + 2:]
    width = own[0].shape[1]
    tile = own[0].shape[2]
    step = pl.program_id(0)
    for n in range(count):
        for c in range(2):
            rhs[cols_ref[n], :, c * tile:(c + 1) * tile] = other[n][c]
    weights = rhs[...].reshape(PLANE * width, 2 * tile)
    mid = lags // 2

    def put(slot, t, real, imag):
        mod[slot, t * width:(t + 1) * width, :tile] = real.astype(jnp.bfloat16)
        mod[slot, t * width:(t + 1) * width, tile:] = imag.astype(jnp.bfloat16)

    for m in range(PLANE):
        slot = m % 2
        real, imag = own[m][0].astype(jnp.float32), own[m][1].astype(jnp.float32)
        for lag in range(mid + 1):
            cosine = cos_ref[lag:lag + 1, :]
            sine = sin_ref[lag:lag + 1, :]
            rc, rs, ic, im = real * cosine, real * sine, imag * cosine, imag * sine
            put(slot, mid - lag, rc + im, ic - rs)
            if 0 < lag < lags - mid:
                put(slot, mid + lag, rc - im, ic + rs)
        part = lax.dot_general(
            mod[slot], weights, (((1,), (1,)), ((), ())), preferred_element_type=jnp.float32
        )

        @pl.when(step == 0)
        def _():
            acc[m] = part

        @pl.when(step > 0)
        def _():
            acc[m] += part

    @pl.when(step == steps - 1)
    def _():
        for m in range(PLANE):
            for j in range(first, PLANE):
                for t in range(0, lags, 2):
                    pair = [
                        acc[m, u * width:(u + 1) * width, j * width:(j + 1) * width]
                        for u in (t, t + 1)
                    ]
                    outs[m][j - first, :, t * width:(t + 2) * width] = jnp.concatenate(pair, 1)


def pair_products(own, other, cols, half, tables, lags, first):
    _, width, bins = own[0].shape
    tile = min(512, bins)
    steps = bins // tile
    count = len(other)
    block = pl.BlockSpec((2, width, tile), lambda f, cols, half: (0, 0, f))
    table = pl.BlockSpec((8, tile), lambda f, cols, half: (0, half[0] * steps + f))
    shape = (PLANE - first, width, lags * width)
    return pl.pallas_call(
        functools.partial(pair_kernel, lags, steps, first, count),
        out_shape=[jax.ShapeDtypeStruct(shape, jnp.float32)] * PLANE,
        grid_spec=pltpu.PrefetchScalarGridSpec(
            num_scalar_prefetch=2,
            grid=(steps,),
            in_specs=[block] * (PLANE + count) + [table] * 2,
            out_specs=[pl.BlockSpec(shape, lambda f, cols, half: (0, 0, 0))] * PLANE,
            scratch_shapes=[
                pltpu.VMEM((PLANE, width, 2 * tile), jnp.bfloat16),
                pltpu.VMEM((2, lags * width, 2 * tile), jnp.bfloat16),
                pltpu.VMEM((PLANE, lags * width, PLANE * width), jnp.float32),
            ],
        ),
        compiler_params=pltpu.CompilerParams(vmem_limit_bytes=40 * 1024 * 1024),
        cost_estimate=pl.CostEstimate(
            flops=2 * PLANE * lags * width * PLANE * width * 2 * bins,
            bytes_accessed=4 * 4 * 2 * width * bins + 4 * PLANE * width * lags * width,
            transcendentals=0,
        ),
    )(cols, half, *own, *other, *tables)


def final_kernel(norm, q_ref, flags_ref, *refs):
    same, near, far = refs[0:3], refs[3:6], refs[6:9]
    out = refs[9]
    q = q_ref[0]

    def emit(parts, j, d):
        scale = flags_ref[d].astype(jnp.float32) * norm
        out[0, d] = (parts[0][j] + parts[1][j] + parts[2][j]) * scale

    for j in range(PLANE):
        emit(near, j, PLANE + q - j)

        @pl.when(j <= q)
        def _():
            emit(same, j, q - j)

        if j > 0:
            @pl.when(j > q)
            def _():
                scale = flags_ref[2 * PLANE + q - j].astype(jnp.float32) * norm
                out[0, 2 * PLANE + q - j] = (far[0][j - 1] + far[1][j - 1] + far[2][j - 1]) * scale


def per_device(spectra, pair_valid):
    own = spectra[0]
    segments, _, width, bins = own.shape
    steps = pair_valid.shape[1]
    lags = 8
    ring = 2 * steps
    stride = lax.axis_size("chan") // ring
    place = lax.axis_index("chan") // stride
    q = lax.rem(place, PLANE)
    y, c = q // 2, lax.rem(q, 2)
    half_bins = bins // 2
    norm = 1.0 / math.sqrt(2.0 * segments * bins)
    tables = [jnp.asarray(t) for t in lag_rows(bins, lags)]

    def move(value, to):
        pairs = [
            (r * stride + s, to(r) * stride + s) for r in range(ring) for s in range(stride)
        ]
        return lax.ppermute(value, "chan", pairs)

    def to_plane(k):
        return lambda r: r - r % PLANE + ((r % PLANE) ^ k)

    def up(r):
        return (r + PLANE) % ring

    def piece(k):
        s = y ^ (k >> 1)
        h = c ^ (k & 1)
        return lax.dynamic_slice(own, (s, 0, 0, h * half_bins), (1, 2, width, half_bins))[0]

    sib = move(piece(1), to_plane(1))
    mine = piece(0)
    cross = move(piece(2), to_plane(2))
    diag = move(piece(3), to_plane(3))
    here = [mine, sib, cross, diag]
    near = [move(x, up) for x in here]
    odd = c == 1
    low = y == 0
    first_send = jnp.where(odd, near[0], near[1])
    even_send = jnp.where(odd, near[1], near[0])
    second_send = jnp.where(low, near[2], even_send)
    third_send = jnp.where(low, near[3], jnp.where(odd, near[2], near[3]))
    far = [move(x, up) for x in (first_send, second_send, third_send)]

    slots = jnp.stack([q ^ k for k in range(PLANE)]).astype(jnp.int32)
    far_slots = jnp.stack([
        jnp.where(low, 1, 3), jnp.where(low, q ^ 2, 2), jnp.where(low, q ^ 3, 1)
    ]).astype(jnp.int32)
    half = c.astype(jnp.int32)[None]

    def reduced(parts):
        from_sib = move(parts[1], to_plane(1))
        pass_on = parts[2] + move(parts[3], to_plane(1))
        return [parts[0], from_sib, move(pass_on, to_plane(2))]

    same_sum = reduced(pair_products(here, here, slots, half, tables, lags, 0))
    near_sum = reduced(pair_products(here, near, slots, half, tables, lags, 0))
    far_sum = reduced(pair_products(here, far, far_slots, half, tables, lags, 1))

    return pl.pallas_call(
        functools.partial(final_kernel, norm),
        out_shape=jax.ShapeDtypeStruct((1, steps, width, lags * width), jnp.float32),
        in_specs=[pl.BlockSpec(memory_space=pltpu.SMEM)] * 2
        + [pl.BlockSpec(memory_space=pltpu.VMEM)] * 9,
        out_specs=pl.BlockSpec(memory_space=pltpu.VMEM),
        compiler_params=pltpu.CompilerParams(vmem_limit_bytes=40 * 1024 * 1024),
    )(q.astype(jnp.int32)[None], pair_valid[0], *same_sum, *near_sum, *far_sum)


def solution(mesh):
    return jax.shard_map(
        per_device,
        mesh=mesh,
        in_specs=(P(("groups", "chan"), None, None, None, None), P(("groups", "chan"), None)),
        out_specs=P(("groups", "chan"), None, None, None),
        check_vma=False,
    )
```

```python
import functools
import math

import jax
import jax.numpy as jnp
import ml_dtypes
import numpy as np
from jax import lax
from jax.experimental import pallas as pl
from jax.experimental.pallas import tpu as pltpu
from jax.sharding import PartitionSpec as P

PLANE = 4
LAGS = 8
MID = LAGS // 2
TILE = 512
LIMIT = 40 * 1024 * 1024


def lag_rows(bins):
    rows = np.arange(8)[:, None]
    phase = np.mod(np.arange(bins)[None, :] * rows, 2 * bins)
    angle = phase.astype(np.float64) * (math.pi / bins)

    def rounded(x):
        return x.astype(np.float32).astype(ml_dtypes.bfloat16).astype(np.float32)

    return rounded(np.cos(angle)), rounded(np.sin(angle))


def modulate_into(mod, real_imag, half, cos_ref, sin_ref):
    _, width, bins = real_imag.shape
    for f in range(0, bins, TILE):
        here = slice(f, f + TILE)
        there = slice(bins + f, bins + f + TILE)
        table = pl.ds(pl.multiple_of(half * bins + f, TILE), TILE)
        real = real_imag[0, :, here].astype(jnp.float32)
        imag = real_imag[1, :, here].astype(jnp.float32)
        for lag in range(MID + 1):
            cosine = cos_ref[lag:lag + 1, table]
            sine = sin_ref[lag:lag + 1, table]
            rc, rs, ic, im = real * cosine, real * sine, imag * cosine, imag * sine
            low = slice((MID - lag) * width, (MID - lag + 1) * width)
            mod[low, here] = (rc + im).astype(jnp.bfloat16)
            mod[low, there] = (ic - rs).astype(jnp.bfloat16)
            if 0 < lag < LAGS - MID:
                high = slice((MID + lag) * width, (MID + lag + 1) * width)
                mod[high, here] = (rc - im).astype(jnp.bfloat16)
                mod[high, there] = (ic + rs).astype(jnp.bfloat16)


def gather_columns(rhs, other, cols_ref):
    _, width, bins = other[0].shape
    for n, ref in enumerate(other):
        row = pl.multiple_of(cols_ref[n] * width, width)
        for c in range(2):
            rhs[pl.ds(row, width), c * bins:(c + 1) * bins] = ref[c]


def product(acc, mod, rhs, outs, width):
    acc[...] = lax.dot_general(
        mod[...], rhs[...], (((1,), (1,)), ((), ())), preferred_element_type=jnp.float32
    )
    places = [out.at[j] for out in outs for j in range(out.shape[0])]
    for j, out in enumerate(places):
        for t in range(0, LAGS, 2):
            pair = [acc[u * width:(u + 1) * width, j * width:(j + 1) * width] for u in (t, t + 1)]
            out[:, t * width:(t + 2) * width] = jnp.concatenate(pair, 1)


def plane_kernel(count, skip, half_ref, rows_ref, cols_ref, *refs):
    here, other, refs = refs[:PLANE], refs[PLANE:PLANE + count], refs[PLANE + count:]
    (cos_ref, sin_ref), outs, (mod, rhs, acc) = refs[:2], refs[2:-3], refs[-3:]
    if not count:
        other = here
    each = len(outs) // PLANE
    width = here[0].shape[1]
    gather_columns(rhs, other, cols_ref)

    def one(m):
        modulate_into(mod.at[m % 2], here[m], half_ref[0], cos_ref, sin_ref)
        product(acc, mod.at[m % 2], rhs, outs[m * each:(m + 1) * each], width)

    for m in range(PLANE):
        if skip is None:
            one(m)
        else:
            pl.when(rows_ref[m] != skip)(functools.partial(one, m))


def last_kernel(half_ref, rows_ref, cols_ref, *refs):
    here, (other, cos_ref, sin_ref, out, mod, rhs, acc) = refs[:PLANE], refs[PLANE:]
    gather_columns(rhs, [other], cols_ref)
    for m in range(PLANE):
        @pl.when(rows_ref[m] == 0)
        def _():
            modulate_into(mod.at[0], here[m], half_ref[0], cos_ref, sin_ref)
    product(acc, mod.at[0], rhs, [out], here[0].shape[1])


def products(here, other, half, rows, cols, tables, skip=None, last=False):
    count = len(other)
    _, width, bins = here[0].shape
    columns = (count or PLANE) * width
    body = last_kernel if last else functools.partial(plane_kernel, count, skip)
    shape = (1 if last else 2, width, LAGS * width)
    outs = [jax.ShapeDtypeStruct(shape, jnp.float32)]
    if not last:
        outs = outs * (PLANE * (count or PLANE) // 2)
    arrays = [*here, *other, *tables]

    def whole(x):
        zeros = (0,) * len(x.shape)
        return pl.BlockSpec(x.shape, lambda *_: zeros)

    return pl.pallas_call(
        body,
        out_shape=outs,
        grid_spec=pltpu.PrefetchScalarGridSpec(
            num_scalar_prefetch=3,
            grid=(1,),
            in_specs=[whole(x) for x in arrays],
            out_specs=[whole(x) for x in outs],
            scratch_shapes=[
                pltpu.VMEM((1 if last else 2, LAGS * width, 2 * bins), jnp.bfloat16),
                pltpu.VMEM((columns, 2 * bins), jnp.bfloat16),
                pltpu.VMEM((LAGS * width, columns), jnp.float32),
            ],
        ),
        compiler_params=pltpu.CompilerParams(vmem_limit_bytes=LIMIT),
        cost_estimate=pl.CostEstimate(flops=1024, bytes_accessed=1024, transcendentals=0),
    )(half, rows, cols, *arrays)


def final_kernel(norm, q_ref, flags_ref, *refs):
    same, near, far, last = refs[0:5], refs[5:10], refs[10:13], refs[13:17]
    out = refs[17]
    q = q_ref[0]

    def emit(total, d):
        out[0, d] = total * (flags_ref[d].astype(jnp.float32) * norm)

    def plane_sum(parts, j):
        each = len(parts) // 2
        n, r = divmod(j, 2)
        return parts[n][r] + parts[each + n][r] + parts[-1][j]

    for j in range(PLANE):
        emit(plane_sum(near, j), PLANE + q - j)

        @pl.when(j <= q)
        def _():
            emit(plane_sum(same, j), q - j)

    for j in (2, 3):
        @pl.when(j > q)
        def _():
            emit(plane_sum(far, j - 2), 2 * PLANE + q - j)

    @pl.when(q == 0)
    def _():
        emit(last[0][0] + last[1][0] + last[2][0] + last[3][0], 2 * PLANE - 1)


def per_device(spectra, pair_valid):
    own = spectra[0]
    segments, _, width, bins = own.shape
    steps = pair_valid.shape[1]
    ring = 2 * steps
    stride = lax.axis_size("chan") // ring
    place = lax.axis_index("chan") // stride
    q = lax.rem(place, PLANE).astype(jnp.int32)
    y, c = q // 2, lax.rem(q, 2)
    half_bins = bins // 2
    norm = 1.0 / math.sqrt(2.0 * segments * bins)
    tables = [jnp.asarray(t) for t in lag_rows(bins)]

    def move(value, to, only=None):
        pairs = [
            (r * stride + s, to(r) * stride + s)
            for r in range(ring) if only is None or r % PLANE == only for s in range(stride)
        ]
        return lax.ppermute(value, "chan", pairs)

    def to_plane(k):
        return lambda r: r - r % PLANE + ((r % PLANE) ^ k)

    def up(r):
        return (r + PLANE) % ring

    def ints(*values):
        return jnp.stack([jnp.asarray(v, jnp.int32) for v in values])

    def piece(block, k):
        s = y ^ (k >> 1)
        h = c ^ (k & 1)
        return lax.dynamic_slice(block, (s, 0, 0, h * half_bins), (1, 2, width, half_bins))[0]

    def after(values, *others):
        return lax.optimization_barrier((*values, *others))[:len(values)]

    def in_core(parts):
        each = len(parts) // PLANE
        rows = [parts[m * each:(m + 1) * each] for m in range(PLANE)]
        got = [[move(x, to_plane(1)) for x in row] for row in rows[1::2]]
        passed = [a + b for a, b in zip(rows[2], got[1])]
        return rows[0], got[0], jnp.concatenate(passed, 0)

    def across(sums):
        return [*sums[0], *sums[1], move(sums[2], to_plane(2))]

    slots = ints(*[q ^ k for k in range(PLANE)])

    mine = piece(own, 0)
    (rest,) = after([own], mine)
    near0 = move(mine, up)
    sib, cross, diag = [move(piece(rest, k), to_plane(k)) for k in range(1, PLANE)]
    near1 = move(sib, up)
    (cross,) = after([cross], near0)
    near2 = move(cross, up)
    (diag,) = after([diag], near1)
    near3 = move(diag, up)
    here = [mine, sib, cross, diag]
    near = [near0, near1, near2, near3]
    half = ints(c)
    same_core = in_core(products(here, [], half, slots, slots, tables))
    same_sum = across(same_core)

    odd = c == 1
    low = y == 0
    far = [move(jnp.where(low, near2, near0), up)]
    send = jnp.where(low, near3, near1)
    far.append(move(send, up))
    a, b, d, e = after(near, send)
    last_send = jnp.where(low, jnp.where(odd, a, b), jnp.where(odd, d, e))
    last = move(last_send, up)

    near_core = in_core(
        products(here, after(near, same_core[2], last_send), half, slots, slots, tables)
    )
    near_sum = across(near_core)
    far_core = in_core(products(
        here, after(far, near_core[2], same_sum[2]), half, slots, ints(c, 1 - c), tables,
        skip=PLANE - 1,
    ))
    far_sum = across(far_core)
    (last_part,) = products(
        here, after([last], far_core[2]), half, slots, ints(0), tables, last=True
    )
    last_sum = [last_part] + [move(last_part, to_plane(k), k) for k in (1, 2, 3)]

    return pl.pallas_call(
        functools.partial(final_kernel, norm),
        out_shape=jax.ShapeDtypeStruct((1, steps, width, LAGS * width), jnp.float32),
        in_specs=[pl.BlockSpec(memory_space=pltpu.SMEM)] * 2
        + [pl.BlockSpec(memory_space=pltpu.VMEM)] * 17,
        out_specs=pl.BlockSpec(memory_space=pltpu.VMEM),
        compiler_params=pltpu.CompilerParams(vmem_limit_bytes=LIMIT),
    )(ints(q), pair_valid[0], *same_sum, *near_sum, *far_sum, *last_sum)


def solution(mesh):
    return jax.shard_map(
        per_device,
        mesh=mesh,
        in_specs=(P(("groups", "chan"), None, None, None, None), P(("groups", "chan"), None)),
        out_specs=P(("groups", "chan"), None, None, None),
        check_vma=False,
    )
```

```python
import functools
import math

import jax
import jax.numpy as jnp
import ml_dtypes
import numpy as np
from jax import lax
from jax.experimental import pallas as pl
from jax.experimental.pallas import tpu as pltpu
from jax.sharding import PartitionSpec as P

PLANE = 4
LAGS = 8
MID = LAGS // 2
TILE = 512
LIMIT = 40 * 1024 * 1024


def lag_rows(bins):
    rows = np.arange(8)[:, None]
    phase = np.mod(np.arange(bins)[None, :] * rows, 2 * bins)
    angle = phase.astype(np.float64) * (math.pi / bins)

    def rounded(x):
        return x.astype(np.float32).astype(ml_dtypes.bfloat16).astype(np.float32)

    return rounded(np.cos(angle)), rounded(np.sin(angle))


def modulate_into(mod, real_imag, half, cos_ref, sin_ref):
    _, width, bins = real_imag.shape
    for f in range(0, bins, TILE):
        here = slice(f, f + TILE)
        there = slice(bins + f, bins + f + TILE)
        table = pl.ds(pl.multiple_of(half * bins + f, TILE), TILE)
        real = real_imag[0, :, here].astype(jnp.float32)
        imag = real_imag[1, :, here].astype(jnp.float32)
        for lag in range(MID + 1):
            cosine = cos_ref[lag:lag + 1, table]
            sine = sin_ref[lag:lag + 1, table]
            rc, rs, ic, im = real * cosine, real * sine, imag * cosine, imag * sine
            low = slice((MID - lag) * width, (MID - lag + 1) * width)
            mod[low, here] = (rc + im).astype(jnp.bfloat16)
            mod[low, there] = (ic - rs).astype(jnp.bfloat16)
            if 0 < lag < LAGS - MID:
                high = slice((MID + lag) * width, (MID + lag + 1) * width)
                mod[high, here] = (rc - im).astype(jnp.bfloat16)
                mod[high, there] = (ic + rs).astype(jnp.bfloat16)


def gather_columns(rhs, other, cols_ref):
    _, width, bins = other[0].shape
    for n, ref in enumerate(other):
        row = pl.multiple_of(cols_ref[n] * width, width)
        for c in range(2):
            rhs[pl.ds(row, width), c * bins:(c + 1) * bins] = ref[c]


def product(acc, mod, rhs, outs, width):
    acc[...] = lax.dot_general(
        mod[...], rhs[...], (((1,), (1,)), ((), ())), preferred_element_type=jnp.float32
    )
    places = [out.at[j] for out in outs for j in range(out.shape[0])]
    for j, out in enumerate(places):
        for t in range(0, LAGS, 2):
            pair = [acc[u * width:(u + 1) * width, j * width:(j + 1) * width] for u in (t, t + 1)]
            out[:, t * width:(t + 2) * width] = jnp.concatenate(pair, 1)


def plane_kernel(count, skip, copies, half_ref, rows_ref, cols_ref, *refs):
    here, other, refs = refs[:PLANE], refs[PLANE:PLANE + count], refs[PLANE + count:]
    (cos_ref, sin_ref), (mod, rhs, acc) = refs[:2], refs[-3:]
    n = PLANE * (count or PLANE) // 2 + copies
    outs = refs[-3 - n:-3]
    for k in range(copies):
        outs[n - copies + k][...] = refs[2 + k][...]
    outs = outs[:n - copies]
    if not count:
        other = here
    each = len(outs) // PLANE
    width = here[0].shape[1]
    gather_columns(rhs, other, cols_ref)

    def one(m):
        modulate_into(mod.at[m % 2], here[m], half_ref[0], cos_ref, sin_ref)
        product(acc, mod.at[m % 2], rhs, outs[m * each:(m + 1) * each], width)

    for m in range(PLANE):
        if skip is None:
            one(m)
        else:
            pl.when(rows_ref[m] != skip)(functools.partial(one, m))


def last_kernel(half_ref, rows_ref, cols_ref, *refs):
    here, (other, cos_ref, sin_ref) = refs[:PLANE], refs[PLANE:PLANE + 3]
    out, mod, rhs, acc = refs[-4:]
    gather_columns(rhs, [other], cols_ref)
    for m in range(PLANE):
        @pl.when(rows_ref[m] == 0)
        def _():
            modulate_into(mod.at[0], here[m], half_ref[0], cos_ref, sin_ref)
    product(acc, mod.at[0], rhs, [out], here[0].shape[1])


def products(here, other, half, rows, cols, tables, skip=None, last=False, copy=(), before=()):
    count = len(other)
    _, width, bins = here[0].shape
    columns = (count or PLANE) * width
    body = last_kernel if last else functools.partial(plane_kernel, count, skip, len(copy))
    shape = (1 if last else 2, width, LAGS * width)
    outs = [jax.ShapeDtypeStruct(shape, jnp.float32)]
    if not last:
        outs = outs * (PLANE * (count or PLANE) // 2)
    outs += [jax.ShapeDtypeStruct(x.shape, x.dtype) for x in copy]
    arrays = [*here, *other, *tables, *copy]

    def whole(x):
        zeros = (0,) * len(x.shape)
        return pl.BlockSpec(x.shape, lambda *_: zeros)

    return pl.pallas_call(
        body,
        out_shape=outs,
        grid_spec=pltpu.PrefetchScalarGridSpec(
            num_scalar_prefetch=3,
            grid=(1,),
            in_specs=[whole(x) for x in arrays]
            + [pl.BlockSpec(memory_space=pl.ANY)] * len(before),
            out_specs=[whole(x) for x in outs],
            scratch_shapes=[
                pltpu.VMEM((1 if last else 2, LAGS * width, 2 * bins), jnp.bfloat16),
                pltpu.VMEM((columns, 2 * bins), jnp.bfloat16),
                pltpu.VMEM((LAGS * width, columns), jnp.float32),
            ],
        ),
        compiler_params=pltpu.CompilerParams(vmem_limit_bytes=LIMIT),
        cost_estimate=pl.CostEstimate(flops=1024, bytes_accessed=1024, transcendentals=0),
    )(half, rows, cols, *arrays, *before)


def final_kernel(norm, q_ref, flags_ref, *refs):
    same, near, far, last = refs[0:5], refs[5:10], refs[10:13], refs[13:17]
    out = refs[17]
    q = q_ref[0]

    def emit(total, d):
        out[0, d] = total * (flags_ref[d].astype(jnp.float32) * norm)

    def plane_sum(parts, j):
        each = len(parts) // 2
        n, r = divmod(j, 2)
        return parts[n][r] + parts[each + n][r] + parts[-1][j]

    for j in range(PLANE):
        emit(plane_sum(near, j), PLANE + q - j)

        @pl.when(j <= q)
        def _():
            emit(plane_sum(same, j), q - j)

    for j in (2, 3):
        @pl.when(j > q)
        def _():
            emit(plane_sum(far, j - 2), 2 * PLANE + q - j)

    @pl.when(q == 0)
    def _():
        emit(last[0][0] + last[1][0] + last[2][0] + last[3][0], 2 * PLANE - 1)


def per_device(spectra, pair_valid):
    own = spectra[0]
    segments, _, width, bins = own.shape
    steps = pair_valid.shape[1]
    ring = 2 * steps
    stride = lax.axis_size("chan") // ring
    place = lax.axis_index("chan") // stride
    q = lax.rem(place, PLANE).astype(jnp.int32)
    y, c = q // 2, lax.rem(q, 2)
    half_bins = bins // 2
    norm = 1.0 / math.sqrt(2.0 * segments * bins)
    tables = [jnp.asarray(t) for t in lag_rows(bins)]

    def move(value, to, only=None):
        pairs = [
            (r * stride + s, to(r) * stride + s)
            for r in range(ring) if only is None or r % PLANE == only for s in range(stride)
        ]
        return lax.ppermute(value, "chan", pairs)

    def to_plane(k):
        return lambda r: r - r % PLANE + ((r % PLANE) ^ k)

    def up(r):
        return (r + PLANE) % ring

    def ints(*values):
        return jnp.stack([jnp.asarray(v, jnp.int32) for v in values])

    def piece(block, k):
        s = y ^ (k >> 1)
        h = c ^ (k & 1)
        return lax.dynamic_slice(block, (s, 0, 0, h * half_bins), (1, 2, width, half_bins))[0]

    def after(values, *others):
        return lax.optimization_barrier((*values, *others))[:len(values)]

    def in_core(parts):
        each = len(parts) // PLANE
        rows = [parts[m * each:(m + 1) * each] for m in range(PLANE)]
        got = [[move(x, to_plane(1)) for x in row] for row in rows[1::2]]
        passed = [a + b for a, b in zip(rows[2], got[1])]
        return rows[0], got[0], jnp.concatenate(passed, 0)

    def across(sums):
        return [*sums[0], *sums[1], move(sums[2], to_plane(2))]

    slots = ints(*[q ^ k for k in range(PLANE)])

    mine = piece(own, 0)
    rest = own
    near0 = move(mine, up)
    sib, cross, diag = [move(piece(rest, k), to_plane(k)) for k in range(1, PLANE)]
    near1 = move(sib, up)
    (cross,) = after([cross], near0)
    near2 = move(cross, up)
    (diag,) = after([diag], near1)
    near3 = move(diag, up)
    here = [mine, sib, cross, diag]
    near = [near0, near1, near2, near3]
    half = ints(c)
    same_core = in_core(products(here, [], half, slots, slots, tables))
    same_sum = across(same_core)

    odd = c == 1
    low = y == 0
    far = [move(jnp.where(low, near2, near0), up)]
    send = jnp.where(low, near3, near1)
    far.append(move(send, up))
    a, b, d, e = after(near, send)
    last_send = jnp.where(low, jnp.where(odd, a, b), jnp.where(odd, d, e))
    last = move(last_send, up)

    near_core = in_core(
        products(here, near, half, slots, slots, tables, before=[same_sum[-1], last_send])
    )
    near_sum = across(near_core)
    far_core = in_core(products(
        here, far, half, slots, ints(c, 1 - c), tables,
        skip=PLANE - 1, before=[near_core[2]],
    ))
    far_sum = across(far_core)
    (last_part,) = products(
        here, [last], half, slots, ints(0), tables, last=True,
        before=[far_core[2], near_sum[-1]],
    )
    last_sum = [last_part] + [move(last_part, to_plane(k), k) for k in (1, 2, 3)]

    return pl.pallas_call(
        functools.partial(final_kernel, norm),
        out_shape=jax.ShapeDtypeStruct((1, steps, width, LAGS * width), jnp.float32),
        in_specs=[pl.BlockSpec(memory_space=pltpu.SMEM)] * 2
        + [pl.BlockSpec(memory_space=pltpu.VMEM)] * 17,
        out_specs=pl.BlockSpec(memory_space=pltpu.VMEM),
        compiler_params=pltpu.CompilerParams(vmem_limit_bytes=LIMIT),
    )(ints(q), pair_valid[0], *same_sum, *near_sum, *far_sum, *last_sum)


def solution(mesh):
    return jax.shard_map(
        per_device,
        mesh=mesh,
        in_specs=(P(("groups", "chan"), None, None, None, None), P(("groups", "chan"), None)),
        out_specs=P(("groups", "chan"), None, None, None),
        check_vma=False,
    )
```

```python
import functools
import math

import jax
import jax.numpy as jnp
import ml_dtypes
import numpy as np
from jax import lax
from jax.experimental import pallas as pl
from jax.experimental.pallas import tpu as pltpu
from jax.sharding import PartitionSpec as P

PLANE = 4
LAGS = 8
MID = LAGS // 2
TILE = 512
LIMIT = 40 * 1024 * 1024


def lag_rows(bins):
    rows = np.arange(8)[:, None]
    phase = np.mod(np.arange(bins)[None, :] * rows, 2 * bins)
    angle = phase.astype(np.float64) * (math.pi / bins)

    def rounded(x):
        return x.astype(np.float32).astype(ml_dtypes.bfloat16).astype(np.float32)

    return rounded(np.cos(angle)), rounded(np.sin(angle))


def modulate_into(mod, real_imag, half, cos_ref, sin_ref):
    _, width, bins = real_imag.shape
    for f in range(0, bins, TILE):
        here = slice(f, f + TILE)
        there = slice(bins + f, bins + f + TILE)
        table = pl.ds(pl.multiple_of(half * bins + f, TILE), TILE)
        real = real_imag[0, :, here].astype(jnp.float32)
        imag = real_imag[1, :, here].astype(jnp.float32)
        for lag in range(MID + 1):
            cosine = cos_ref[lag:lag + 1, table]
            sine = sin_ref[lag:lag + 1, table]
            rc, rs, ic, im = real * cosine, real * sine, imag * cosine, imag * sine
            low = slice((MID - lag) * width, (MID - lag + 1) * width)
            mod[low, here] = (rc + im).astype(jnp.bfloat16)
            mod[low, there] = (ic - rs).astype(jnp.bfloat16)
            if 0 < lag < LAGS - MID:
                high = slice((MID + lag) * width, (MID + lag + 1) * width)
                mod[high, here] = (rc - im).astype(jnp.bfloat16)
                mod[high, there] = (ic + rs).astype(jnp.bfloat16)


def gather_columns(rhs, other, cols_ref):
    _, width, bins = other[0].shape
    for n, ref in enumerate(other):
        row = pl.multiple_of(cols_ref[n] * width, width)
        for c in range(2):
            rhs[pl.ds(row, width), c * bins:(c + 1) * bins] = ref[c]


def product(acc, mod, rhs, outs, width):
    acc[...] = lax.dot_general(
        mod[...], rhs[...], (((1,), (1,)), ((), ())), preferred_element_type=jnp.float32
    )
    emit(acc, outs, width)


def emit(acc, outs, width):
    places = [out.at[j] for out in outs for j in range(out.shape[0])]
    for j, out in enumerate(places):
        for t in range(0, LAGS, 2):
            pair = [acc[u * width:(u + 1) * width, j * width:(j + 1) * width] for u in (t, t + 1)]
            out[:, t * width:(t + 2) * width] = jnp.concatenate(pair, 1)


def plane_kernel(count, skip, lead, half_ref, rows_ref, cols_ref, *refs):
    here, other, refs = refs[:PLANE], refs[PLANE:PLANE + count], refs[PLANE + count:]
    (cos_ref, sin_ref), (mod, rhs, acc) = refs[:2], refs[-3:]
    n = PLANE * (count or PLANE) // 2 + lead
    outs = refs[-3 - n:-3]
    if lead:
        for m in range(PLANE):
            @pl.when(rows_ref[m] == 0)
            def _():
                outs[-1][...] = here[m][...]
    if not count:
        other = here
    each = len(outs) // PLANE
    width = here[0].shape[1]
    gather_columns(rhs, other, cols_ref)

    def one(m):
        modulate_into(mod.at[m % 2], here[m], half_ref[0], cos_ref, sin_ref)
        product(acc, mod.at[m % 2], rhs, outs[m * each:(m + 1) * each], width)

    for m in range(PLANE):
        if skip is None:
            one(m)
        else:
            pl.when(rows_ref[m] != skip)(functools.partial(one, m))


def last_kernel(half_ref, lead, other, cos_ref, sin_ref, *refs):
    out, mod, rhs, acc = refs[-4:]
    _, width, tile = lead.shape
    step = pl.program_id(0)
    for c in range(2):
        rhs[:, c * tile:(c + 1) * tile] = other[c]
    modulate_into(mod, lead, 0, cos_ref, sin_ref)
    part = lax.dot_general(
        mod[...], rhs[...], (((1,), (1,)), ((), ())), preferred_element_type=jnp.float32
    )

    @pl.when(step == 0)
    def _():
        acc[...] = part

    @pl.when(step > 0)
    def _():
        acc[...] += part

    @pl.when(step == pl.num_programs(0) - 1)
    def _():
        emit(acc, [out], width)


def last_product(lead, other, half, tables, before):
    _, width, bins = lead.shape
    steps = bins // TILE
    tile = pl.BlockSpec((2, width, TILE), lambda f, half: (0, 0, f))
    table = pl.BlockSpec((8, TILE), lambda f, half: (0, half[0] * steps + f))
    shape = (1, width, LAGS * width)
    return pl.pallas_call(
        last_kernel,
        out_shape=jax.ShapeDtypeStruct(shape, jnp.float32),
        grid_spec=pltpu.PrefetchScalarGridSpec(
            num_scalar_prefetch=1,
            grid=(steps,),
            in_specs=[tile, tile, table, table]
            + [pl.BlockSpec(memory_space=pl.ANY)] * len(before),
            out_specs=pl.BlockSpec(shape, lambda f, half: (0, 0, 0)),
            scratch_shapes=[
                pltpu.VMEM((LAGS * width, 2 * TILE), jnp.bfloat16),
                pltpu.VMEM((width, 2 * TILE), jnp.bfloat16),
                pltpu.VMEM((LAGS * width, width), jnp.float32),
            ],
        ),
        compiler_params=pltpu.CompilerParams(vmem_limit_bytes=LIMIT),
        cost_estimate=pl.CostEstimate(flops=1024, bytes_accessed=1024, transcendentals=0),
    )(half, lead, other, *tables, *before)


def products(here, other, half, rows, cols, tables, skip=None, lead=False, before=()):
    count = len(other)
    _, width, bins = here[0].shape
    columns = (count or PLANE) * width
    body = functools.partial(plane_kernel, count, skip, lead)
    shape = (2, width, LAGS * width)
    outs = [jax.ShapeDtypeStruct(shape, jnp.float32)] * (PLANE * (count or PLANE) // 2)
    if lead:
        outs.append(jax.ShapeDtypeStruct(here[0].shape, here[0].dtype))
    arrays = [*here, *other, *tables]

    def whole(x):
        zeros = (0,) * len(x.shape)
        return pl.BlockSpec(x.shape, lambda *_: zeros)

    return pl.pallas_call(
        body,
        out_shape=outs,
        grid_spec=pltpu.PrefetchScalarGridSpec(
            num_scalar_prefetch=3,
            grid=(1,),
            in_specs=[whole(x) for x in arrays]
            + [pl.BlockSpec(memory_space=pl.ANY)] * len(before),
            out_specs=[whole(x) for x in outs],
            scratch_shapes=[
                pltpu.VMEM((2, LAGS * width, 2 * bins), jnp.bfloat16),
                pltpu.VMEM((columns, 2 * bins), jnp.bfloat16),
                pltpu.VMEM((LAGS * width, columns), jnp.float32),
            ],
        ),
        compiler_params=pltpu.CompilerParams(vmem_limit_bytes=LIMIT),
        cost_estimate=pl.CostEstimate(flops=1024, bytes_accessed=1024, transcendentals=0),
    )(half, rows, cols, *arrays, *before)


def gate_kernel(given, *refs):
    for n in range(given.shape[0]):
        refs[-1][n] = given[n]


def gate(scalars, others, weight):
    return pl.pallas_call(
        gate_kernel,
        out_shape=jax.ShapeDtypeStruct(scalars.shape, jnp.int32),
        in_specs=[pl.BlockSpec(memory_space=pltpu.SMEM)]
        + [pl.BlockSpec(memory_space=pl.ANY)] * len(others),
        out_specs=pl.BlockSpec(memory_space=pltpu.SMEM),
        cost_estimate=pl.CostEstimate(flops=weight, bytes_accessed=1024, transcendentals=0),
    )(scalars, *others)


def final_kernel(norm, q_ref, flags_ref, *refs):
    same, near, far, last = refs[0:5], refs[5:10], refs[10:13], refs[13:17]
    out = refs[17]
    q = q_ref[0]

    def emit(total, d):
        out[0, d] = total * (flags_ref[d].astype(jnp.float32) * norm)

    def plane_sum(parts, j):
        each = len(parts) // 2
        n, r = divmod(j, 2)
        return parts[n][r] + parts[each + n][r] + parts[-1][j]

    for j in range(PLANE):
        emit(plane_sum(near, j), PLANE + q - j)

        @pl.when(j <= q)
        def _():
            emit(plane_sum(same, j), q - j)

    for j in (2, 3):
        @pl.when(j > q)
        def _():
            emit(plane_sum(far, j - 2), 2 * PLANE + q - j)

    @pl.when(q == 0)
    def _():
        emit(last[0][0] + last[1][0] + last[2][0] + last[3][0], 2 * PLANE - 1)


def per_device(spectra, pair_valid):
    own = spectra[0]
    segments, _, width, bins = own.shape
    steps = pair_valid.shape[1]
    ring = 2 * steps
    stride = lax.axis_size("chan") // ring
    place = lax.axis_index("chan") // stride
    q = lax.rem(place, PLANE).astype(jnp.int32)
    y, c = q // 2, lax.rem(q, 2)
    half_bins = bins // 2
    norm = 1.0 / math.sqrt(2.0 * segments * bins)
    tables = [jnp.asarray(t) for t in lag_rows(bins)]

    def move(value, to, only=None):
        pairs = [
            (r * stride + s, to(r) * stride + s)
            for r in range(ring) if only is None or r % PLANE == only for s in range(stride)
        ]
        return lax.ppermute(value, "chan", pairs)

    def to_plane(k):
        return lambda r: r - r % PLANE + ((r % PLANE) ^ k)

    def up(r):
        return (r + PLANE) % ring

    def ints(*values):
        return jnp.stack([jnp.asarray(v, jnp.int32) for v in values])

    def piece(block, k):
        s = y ^ (k >> 1)
        h = c ^ (k & 1)
        return lax.dynamic_slice(block, (s, 0, 0, h * half_bins), (1, 2, width, half_bins))[0]

    def after(values, *others):
        return lax.optimization_barrier((*values, *others))[:len(values)]

    def in_core(parts):
        each = len(parts) // PLANE
        rows = [parts[m * each:(m + 1) * each] for m in range(PLANE)]
        got = [[move(x, to_plane(1)) for x in row] for row in rows[1::2]]
        passed = [a + b for a, b in zip(rows[2], got[1])]
        return rows[0], got[0], jnp.concatenate(passed, 0)

    def across(sums):
        return [*sums[0], *sums[1], move(sums[2], to_plane(2))]

    slots = ints(*[q ^ k for k in range(PLANE)])

    mine = piece(own, 0)
    near0 = move(mine, up)
    sib, cross, diag = [move(piece(own, k), to_plane(k)) for k in range(1, PLANE)]
    near1 = move(sib, up)
    (cross,) = after([cross], near0)
    near2 = move(cross, up)
    (diag,) = after([diag], near1)
    near3 = move(diag, up)
    here = [mine, sib, cross, diag]
    near = [near0, near1, near2, near3]
    half = ints(c)
    *parts, lead = products(here, [], half, slots, slots, tables, lead=True, before=[])
    same_core = in_core(parts)
    same_sum = across(same_core)

    odd = c == 1
    low = y == 0
    far = [move(jnp.where(low, near2, near0), up)]
    send = jnp.where(low, near3, near1)
    far.append(move(send, up))
    a, b, d, e = after(near, send)
    last_send = jnp.where(low, jnp.where(odd, a, b), jnp.where(odd, d, e))
    last = move(last_send, up)

    near_core = in_core(
        products(here, near, half, slots, gate(slots, [near0, near1, near2, near3], 9200000000), tables, before=[same_sum[-1], last_send])
    )
    near_sum = across(near_core)
    far_core = in_core(products(
        here, far, half, slots, ints(c, 1 - c), tables,
        skip=PLANE - 1, before=[near_core[2], same_sum[-1]],
    ))
    far_sum = across(far_core)
    last_part = last_product(lead, last, half, tables, [far_core[2], near_sum[-1]])
    last_sum = [last_part] + [move(last_part, to_plane(k), k) for k in (1, 2, 3)]

    return pl.pallas_call(
        functools.partial(final_kernel, norm),
        out_shape=jax.ShapeDtypeStruct((1, steps, width, LAGS * width), jnp.float32),
        in_specs=[pl.BlockSpec(memory_space=pltpu.SMEM)] * 2
        + [pl.BlockSpec(memory_space=pltpu.VMEM)] * 17,
        out_specs=pl.BlockSpec(memory_space=pltpu.VMEM),
        compiler_params=pltpu.CompilerParams(vmem_limit_bytes=LIMIT),
    )(ints(q), pair_valid[0], *same_sum, *near_sum, *far_sum, *last_sum)


def solution(mesh):
    return jax.shard_map(
        per_device,
        mesh=mesh,
        in_specs=(P(("groups", "chan"), None, None, None, None), P(("groups", "chan"), None)),
        out_specs=P(("groups", "chan"), None, None, None),
        check_vma=False,
    )
```

```python
import functools
import math

import jax
import jax.numpy as jnp
import ml_dtypes
import numpy as np
from jax import lax
from jax.experimental import pallas as pl
from jax.experimental.pallas import tpu as pltpu
from jax.sharding import PartitionSpec as P

PLANE = 4
LAGS = 8
MID = LAGS // 2
TILE = 512
FIRST, SECOND = 3_450_000_000, 23_000_000_000
LIMIT = 40 * 1024 * 1024


def lag_rows(bins):
    rows = np.arange(8)[:, None]
    phase = np.mod(np.arange(bins)[None, :] * rows, 2 * bins)
    angle = phase.astype(np.float64) * (math.pi / bins)

    def rounded(x):
        return x.astype(np.float32).astype(ml_dtypes.bfloat16).astype(np.float32)

    return rounded(np.cos(angle)), rounded(np.sin(angle))


def modulate_into(mod, real_imag, half, cos_ref, sin_ref):
    _, width, bins = real_imag.shape
    for f in range(0, bins, TILE):
        here = slice(f, f + TILE)
        there = slice(bins + f, bins + f + TILE)
        table = pl.ds(pl.multiple_of(half * bins + f, TILE), TILE)
        real = real_imag[0, :, here].astype(jnp.float32)
        imag = real_imag[1, :, here].astype(jnp.float32)
        for lag in range(MID + 1):
            cosine = cos_ref[lag:lag + 1, table]
            sine = sin_ref[lag:lag + 1, table]
            rc, rs, ic, im = real * cosine, real * sine, imag * cosine, imag * sine
            low = slice((MID - lag) * width, (MID - lag + 1) * width)
            mod[low, here] = (rc + im).astype(jnp.bfloat16)
            mod[low, there] = (ic - rs).astype(jnp.bfloat16)
            if 0 < lag < LAGS - MID:
                high = slice((MID + lag) * width, (MID + lag + 1) * width)
                mod[high, here] = (rc - im).astype(jnp.bfloat16)
                mod[high, there] = (ic + rs).astype(jnp.bfloat16)


def gather_columns(rhs, other, cols_ref):
    _, width, bins = other[0].shape
    for n, ref in enumerate(other):
        row = pl.multiple_of(cols_ref[n] * width, width)
        for c in range(2):
            rhs[pl.ds(row, width), c * bins:(c + 1) * bins] = ref[c]


def product(acc, mod, rhs, outs, width):
    acc[...] = lax.dot_general(
        mod[...], rhs[...], (((1,), (1,)), ((), ())), preferred_element_type=jnp.float32
    )
    emit(acc, outs, width)


def emit(acc, outs, width):
    places = [out.at[j] for out in outs for j in range(out.shape[0])]
    for j, out in enumerate(places):
        for t in range(0, LAGS, 2):
            pair = [acc[u * width:(u + 1) * width, j * width:(j + 1) * width] for u in (t, t + 1)]
            out[:, t * width:(t + 2) * width] = jnp.concatenate(pair, 1)


def plane_kernel(count, skip, lead, half_ref, rows_ref, cols_ref, *refs):
    here, other, refs = refs[:PLANE], refs[PLANE:PLANE + count], refs[PLANE + count:]
    (cos_ref, sin_ref), (mod, rhs, acc) = refs[:2], refs[-3:]
    n = PLANE * (count or PLANE) // 2 + lead
    outs = refs[-3 - n:-3]
    if lead:
        for m in range(PLANE):
            @pl.when(rows_ref[m] == 0)
            def _():
                outs[-1][...] = here[m][...]
    if not count:
        other = here
    each = len(outs) // PLANE
    width = here[0].shape[1]
    gather_columns(rhs, other, cols_ref)

    def one(m):
        modulate_into(mod.at[m % 2], here[m], half_ref[0], cos_ref, sin_ref)
        product(acc, mod.at[m % 2], rhs, outs[m * each:(m + 1) * each], width)

    for m in range(PLANE):
        if skip is None:
            one(m)
        else:
            pl.when(rows_ref[m] != skip)(functools.partial(one, m))


def last_kernel(half_ref, lead, other, cos_ref, sin_ref, *refs):
    out, mod, rhs, acc = refs[-4:]
    _, width, tile = lead.shape
    step = pl.program_id(0)
    for c in range(2):
        rhs[:, c * tile:(c + 1) * tile] = other[c]
    modulate_into(mod, lead, 0, cos_ref, sin_ref)
    part = lax.dot_general(
        mod[...], rhs[...], (((1,), (1,)), ((), ())), preferred_element_type=jnp.float32
    )

    @pl.when(step == 0)
    def _():
        acc[...] = part

    @pl.when(step > 0)
    def _():
        acc[...] += part

    @pl.when(step == pl.num_programs(0) - 1)
    def _():
        emit(acc, [out], width)


def last_product(lead, other, half, tables, before):
    _, width, bins = lead.shape
    steps = bins // TILE
    tile = pl.BlockSpec((2, width, TILE), lambda f, half: (0, 0, f))
    table = pl.BlockSpec((8, TILE), lambda f, half: (0, half[0] * steps + f))
    shape = (1, width, LAGS * width)
    return pl.pallas_call(
        last_kernel,
        out_shape=jax.ShapeDtypeStruct(shape, jnp.float32),
        grid_spec=pltpu.PrefetchScalarGridSpec(
            num_scalar_prefetch=1,
            grid=(steps,),
            in_specs=[tile, tile, table, table]
            + [pl.BlockSpec(memory_space=pl.ANY)] * len(before),
            out_specs=pl.BlockSpec(shape, lambda f, half: (0, 0, 0)),
            scratch_shapes=[
                pltpu.VMEM((LAGS * width, 2 * TILE), jnp.bfloat16),
                pltpu.VMEM((width, 2 * TILE), jnp.bfloat16),
                pltpu.VMEM((LAGS * width, width), jnp.float32),
            ],
        ),
        compiler_params=pltpu.CompilerParams(vmem_limit_bytes=LIMIT),
        cost_estimate=pl.CostEstimate(flops=1024, bytes_accessed=1024, transcendentals=0),
    )(half, lead, other, *tables, *before)


def products(here, other, half, rows, cols, tables, skip=None, lead=False, before=()):
    count = len(other)
    _, width, bins = here[0].shape
    columns = (count or PLANE) * width
    body = functools.partial(plane_kernel, count, skip, lead)
    shape = (2, width, LAGS * width)
    outs = [jax.ShapeDtypeStruct(shape, jnp.float32)] * (PLANE * (count or PLANE) // 2)
    if lead:
        outs.append(jax.ShapeDtypeStruct(here[0].shape, here[0].dtype))
    arrays = [*here, *other, *tables]

    def whole(x):
        zeros = (0,) * len(x.shape)
        return pl.BlockSpec(x.shape, lambda *_: zeros)

    return pl.pallas_call(
        body,
        out_shape=outs,
        grid_spec=pltpu.PrefetchScalarGridSpec(
            num_scalar_prefetch=3,
            grid=(1,),
            in_specs=[whole(x) for x in arrays]
            + [pl.BlockSpec(memory_space=pl.ANY)] * len(before),
            out_specs=[whole(x) for x in outs],
            scratch_shapes=[
                pltpu.VMEM((2, LAGS * width, 2 * bins), jnp.bfloat16),
                pltpu.VMEM((columns, 2 * bins), jnp.bfloat16),
                pltpu.VMEM((LAGS * width, columns), jnp.float32),
            ],
        ),
        compiler_params=pltpu.CompilerParams(vmem_limit_bytes=LIMIT),
        cost_estimate=pl.CostEstimate(flops=1024, bytes_accessed=1024, transcendentals=0),
    )(half, rows, cols, *arrays, *before)


def gate_kernel(given, *refs):
    for n in range(given.shape[0]):
        refs[-1][n] = given[n]


def gate(scalars, others, weight):
    return pl.pallas_call(
        gate_kernel,
        out_shape=jax.ShapeDtypeStruct(scalars.shape, jnp.int32),
        in_specs=[pl.BlockSpec(memory_space=pltpu.SMEM)]
        + [pl.BlockSpec(memory_space=pl.ANY)] * len(others),
        out_specs=pl.BlockSpec(memory_space=pltpu.SMEM),
        cost_estimate=pl.CostEstimate(flops=weight, bytes_accessed=1024, transcendentals=0),
    )(scalars, *others)


def plane_sum(parts, j):
    each = len(parts) // 2
    n, r = divmod(j, 2)
    return parts[n][r] + parts[each + n][r] + parts[-1][j]


def early_kernel(norm, q_ref, flags_ref, *refs):
    same, near, out = refs[0:5], refs[5:10], refs[10]
    q = q_ref[0]
    for j in range(PLANE):
        d = PLANE + q - j
        out[0, d] = plane_sum(near, j) * (flags_ref[d].astype(jnp.float32) * norm)

        @pl.when(j <= q)
        def _():
            out[0, q - j] = plane_sum(same, j) * (flags_ref[q - j].astype(jnp.float32) * norm)


def final_kernel(norm, q_ref, flags_ref, _, *refs):
    far, last, (out, buf, sems) = refs[0:3], refs[3:-3], refs[-3:]
    q = q_ref[0]

    def each(act):
        for n, j in enumerate((2, 3, 1)):
            d = 2 * PLANE + q - j
            pl.when(j > q)(functools.partial(act, n, j, d)) if j > 1 else pl.when(q == 0)(
                functools.partial(act, n, j, d)
            )

    def write(n, j, d):
        total = plane_sum(far, j - 2) if j > 1 else sum([x[0] for x in last[1:]], last[0][0])
        buf[n] = total * (flags_ref[d].astype(jnp.float32) * norm)
        pltpu.make_async_copy(buf.at[n], out.at[0, d], sems.at[n]).start()

    def wait(n, j, d):
        pltpu.make_async_copy(buf.at[n], out.at[0, d], sems.at[n]).wait()

    each(write)
    each(wait)


def per_device(spectra, pair_valid):
    own = spectra[0]
    segments, _, width, bins = own.shape
    steps = pair_valid.shape[1]
    ring = 2 * steps
    stride = lax.axis_size("chan") // ring
    place = lax.axis_index("chan") // stride
    q = lax.rem(place, PLANE).astype(jnp.int32)
    y, c = q // 2, lax.rem(q, 2)
    half_bins = bins // 2
    norm = 1.0 / math.sqrt(2.0 * segments * bins)
    tables = [jnp.asarray(t) for t in lag_rows(bins)]

    def move(value, to, only=None):
        pairs = [
            (r * stride + s, to(r) * stride + s)
            for r in range(ring) if only is None or r % PLANE == only for s in range(stride)
        ]
        return lax.ppermute(value, "chan", pairs)

    def to_plane(k):
        return lambda r: r - r % PLANE + ((r % PLANE) ^ k)

    def up(r):
        return (r + PLANE) % ring

    def ints(*values):
        return jnp.stack([jnp.asarray(v, jnp.int32) for v in values])

    def piece(block, k):
        s = y ^ (k >> 1)
        h = c ^ (k & 1)
        return lax.dynamic_slice(block, (s, 0, 0, h * half_bins), (1, 2, width, half_bins))[0]

    def after(values, *others):
        return lax.optimization_barrier((*values, *others))[:len(values)]

    def in_core(parts):
        each = len(parts) // PLANE
        rows = [parts[m * each:(m + 1) * each] for m in range(PLANE)]
        got = [[move(x, to_plane(1)) for x in row] for row in rows[1::2]]
        passed = [a + b for a, b in zip(rows[2], got[1])]
        return rows[0], got[0], jnp.concatenate(passed, 0)

    def across(sums):
        return [*sums[0], *sums[1], move(sums[2], to_plane(2))]

    slots = ints(*[q ^ k for k in range(PLANE)])

    mine = piece(own, 0)
    near0 = move(mine, up)
    sib, cross, diag = [move(piece(own, k), to_plane(k)) for k in range(1, PLANE)]
    near1 = move(sib, up)
    (cross,) = after([cross], near0)
    near2 = move(cross, up)
    (diag,) = after([diag], near1)
    near3 = move(diag, up)
    here = [mine, sib, cross, diag]
    near = [near0, near1, near2, near3]
    half = ints(c)
    *parts, lead = products(
        here, [], half, slots, gate(slots, [near0], FIRST), tables, lead=True
    )
    same_core = in_core(parts)
    same_sum = across(same_core)

    odd = c == 1
    low = y == 0
    far = [move(jnp.where(low, near2, near0), up)]
    send = jnp.where(low, near3, near1)
    far.append(move(send, up))
    a, b, d, e = after(near, send)
    last_send = jnp.where(low, jnp.where(odd, a, b), jnp.where(odd, d, e))
    last = move(last_send, up)

    near_core = in_core(
        products(
            here, near, half, slots, gate(slots, near, SECOND), tables,
            before=[same_sum[-1], last_send],
        )
    )
    near_sum = across(near_core)
    far_core = in_core(products(
        here, far, half, slots, ints(c, 1 - c), tables,
        skip=PLANE - 1, before=[near_core[2], same_sum[-1]],
    ))
    far_sum = across(far_core)
    last_part = last_product(lead, last, half, tables, [far_core[2], near_sum[-1]])
    from_y = move(last_part, to_plane(2), 2) + move(last_part, to_plane(3), 3)
    last_sum = [last_part, move(last_part, to_plane(1), 1), from_y]

    smem = pl.BlockSpec(memory_space=pltpu.SMEM)
    vmem = pl.BlockSpec(memory_space=pltpu.VMEM)
    anywhere = pl.BlockSpec(memory_space=pl.ANY)
    shape = jax.ShapeDtypeStruct((1, steps, width, LAGS * width), jnp.float32)
    params = pltpu.CompilerParams(vmem_limit_bytes=LIMIT)
    early = pl.pallas_call(
        functools.partial(early_kernel, norm),
        out_shape=shape,
        in_specs=[smem] * 2 + [vmem] * 10,
        out_specs=vmem,
        compiler_params=params,
        cost_estimate=pl.CostEstimate(flops=1024, bytes_accessed=1024, transcendentals=0),
    )(ints(q), pair_valid[0], *same_sum, *near_sum)
    return pl.pallas_call(
        functools.partial(final_kernel, norm),
        out_shape=shape,
        in_specs=[smem] * 2 + [anywhere] + [vmem] * 6,
        out_specs=anywhere,
        scratch_shapes=[
            pltpu.VMEM((3, width, LAGS * width), jnp.float32), pltpu.SemaphoreType.DMA((3,))
        ],
        input_output_aliases={2: 0},
        compiler_params=params,
    )(ints(q), pair_valid[0], early, *far_sum, *last_sum)


def solution(mesh):
    return jax.shard_map(
        per_device,
        mesh=mesh,
        in_specs=(P(("groups", "chan"), None, None, None, None), P(("groups", "chan"), None)),
        out_specs=P(("groups", "chan"), None, None, None),
        check_vma=False,
    )
```
